256 devices in a mesh: dp: 32 (over z, y), tensor: 8 (over x, core).
Axes of the slice: x: 4, y: 4, z: 8, core: 2. Of those that a mesh axis runs over, the one named last changes fastest.
Arguments:
- grad_a_parts: bfloat16 [32, 32, 5120, 64], P('dp', None, 'tensor'), may hold values from -6 to 6
- grad_b_parts: bfloat16 [32, 32, 64, 8192], P('dp', None, None, 'tensor'), may hold values from -6 to 6
- adapter_a: float32 [32, 5120, 64], P('dp', 'tensor'), may hold values from -0.078125 to 0.078125
- adapter_b: float32 [32, 64, 8192], P('dp', None, 'tensor'), may hold values from -0.75 to 0.75
- moment_a: float32 [32, 5120, 64], P('dp', 'tensor'), may hold values from -8 to 8
- moment_b: float32 [32, 64, 8192], P('dp', None, 'tensor'), may hold values from -8 to 8
- second_a: float32 [32, 5120, 64], P('dp', 'tensor'), may hold values from 0.001 to 0.1
- second_b: float32 [32, 64, 8192], P('dp', None, 'tensor'), may hold values from 0.001 to 0.1
- group_policy: int32 [32, 16], replicated, may hold values from 0 to 31, as said below
- row_slot: int32 [4096], P('dp'), may hold values from 0 to 15, as said below
- cache_length: int32 [4096], P('dp'), may hold values from 1 to 48, as said below
- features: bfloat16 [4096, 5120], P('dp', 'tensor'), may hold values from -6 to 6
- frozen_query_output: bfloat16 [4096, 8192], P('dp', 'tensor'), may hold values from -80 to 80
- kv_cache: bfloat16 [2, 4096, 8, 48, 128], P(None, 'dp', 'tensor'), may hold values from -4 to 4
- new_kv: bfloat16 [2, 4096, 8, 128], P(None, 'dp', 'tensor'), may hold values from -4 to 4
Outputs:
- new_a: float32 [32, 5120, 64], P('dp', 'tensor')
- new_b: float32 [32, 64, 8192], P('dp', None, 'tensor')
- new_moment_a: float32 [32, 5120, 64], P('dp', 'tensor')
- new_moment_b: float32 [32, 64, 8192], P('dp', None, 'tensor')
- new_second_a: float32 [32, 5120, 64], P('dp', 'tensor')
- new_second_b: float32 [32, 64, 8192], P('dp', None, 'tensor')
- attended: bfloat16 [4096, 8192], P('dp', 'tensor')
The draws below stay inside these ranges and needn't reach their ends.
Inputs may be any that keep to these rules, and one draw needn't show every extreme that they name: Each row of group_policy holds 16 different policies in rising order. `row_slot`: within each group of 128 rows the slots never fall; every group's first row has slot 0 and its last row slot 15; no slot of a group is used by more than 16 rows, and slot 0 of every group by exactly 16. `cache_length`: the first row of every group of 128 rows holds 48 positions and its second row one.
All inputs are finite; a program needn't handle non-finite values.
Results may differ from the reference program's by a relative error of at most 0.025.
Values may be sent and summed in bfloat16 or wider, within the bound.
No kernel may reach another device: no remote copies, remote signals or barrier semaphores. Data moves between devices by JAX's collectives and lax.ppermute only.
A program may use at most 128 MiB of HBM per device.

```python
import math
import jax
import jax.numpy as jnp
from jax import lax

D = 5120
KVH = 8
HD = 128
R = 64
ROW_DEV = 128
CACHE = 48
QD = 8192
POLICIES = 32
GROUPS = 32
SLOTS = 16
CAP = 16
ROWS = 4096


def first_keys(key):
    return jnp.clip(jax.random.normal(jax.random.fold_in(key, 21), (ROWS, KVH, HD), jnp.float32), -4.0, 4.0)


def draw_group_policy(key, part):
    key = jax.random.fold_in(key, 1)
    splits = jax.random.split(key, GROUPS)
    perms = jax.vmap(lambda sub: jax.random.permutation(sub, POLICIES))(splits)
    return jnp.sort(perms[:, :SLOTS], axis=1).astype(jnp.int32)


def draw_row_slot(key, part):
    key = jax.random.fold_in(key, 2)
    index = jnp.arange(ROW_DEV)[None, :]
    middle = ROW_DEV - CAP - 1
    if middle <= SLOTS - 1:
        splits = jax.random.split(key, GROUPS)
        perms = jax.vmap(lambda sub: jax.random.permutation(sub, SLOTS - 1))(splits)
        chosen = jnp.sort(perms[:, :middle], axis=1) + 1
        padded = jnp.concatenate([jnp.zeros((GROUPS, CAP), jnp.int32), chosen.astype(jnp.int32), jnp.full((GROUPS, 1), SLOTS - 1, jnp.int32)], axis=1)
        slots = padded
    else:
        offset = jax.random.randint(key, (GROUPS, 1), 0, ROW_DEV)
        slots = jnp.minimum((index * SLOTS + offset) // ROW_DEV, SLOTS - 1)
    slots = jnp.where(index < CAP, 0, slots)
    slots = jnp.where(index == ROW_DEV - 1, SLOTS - 1, slots)
    return slots.reshape(ROWS).astype(jnp.int32)


def draw_cache_length(key, part):
    key = jax.random.fold_in(key, 3)
    lengths = jax.random.randint(key, (ROWS,), 1, CACHE + 1)
    index = jnp.arange(ROWS)
    lengths = jnp.where(index % ROW_DEV == 0, CACHE, lengths)
    lengths = jnp.where(index % ROW_DEV == 1, 1, lengths)
    return lengths.astype(jnp.int32)


def draw_kv_cache(key, part):
    leading = first_keys(key)
    key = jax.random.fold_in(key, 4)
    shape = (2, ROWS, KVH, CACHE, HD)
    fresh = jnp.clip(jax.random.normal(key, shape, jnp.float32), -4.0, 4.0)
    fresh = fresh.at[0, :, :, 0, :].set(leading)
    return fresh.astype(jnp.bfloat16)


def draw_new_kv(key, part):
    key = jax.random.fold_in(key, 5)
    fresh = jnp.clip(jax.random.normal(key, (2, ROWS, KVH, HD), jnp.float32), -4.0, 4.0)
    return fresh.astype(jnp.bfloat16)


def draw_frozen_query_output(key, part):
    key = jax.random.fold_in(key, 6)
    fresh = jnp.clip(jax.random.normal(key, (ROWS, QD), jnp.float32), -6.0, 6.0)
    return fresh.astype(jnp.bfloat16)


def with_spikes(result, rng, source, target, shards_of, factor):
    def block_of(position):
        return (jnp.arange(result.shape[position]) // (result.shape[position] // shards_of)).reshape((-1,) + (1,) * (result.ndim - 1 - position))

    first = jax.random.permutation(rng, shards_of)[block_of(target)]
    other_side = (block_of(target) + shards_of // 2) % shards_of
    return jnp.where((block_of(source) == first) | (block_of(source) == other_side), factor * result, result)


def level_of(key, dims, pieces, least, high):
    level = 1.0
    for axis_at, shards_of in pieces:
        heights = jax.random.uniform(jax.random.fold_in(jax.random.fold_in(key, 6), axis_at), (shards_of,), jnp.float32, least / len(pieces), high / len(pieces))
        level = level * jnp.repeat(jnp.exp(heights), dims[axis_at] // shards_of).reshape((-1,) + (1,) * (len(dims) - 1 - axis_at))
    return level


def noise(stream_key, dims, deviation, bound, cuts=(), held_as=jnp.bfloat16):
    factor_of = level_of(stream_key, dims, cuts, -0.22, 0.18) if cuts else 1.0
    drawn = jax.random.normal(stream_key, dims, jnp.float32) * deviation * factor_of
    return jnp.minimum(jnp.maximum(drawn, -bound), bound).astype(held_as)


def heavy_noise(key, extent, width, reach, shards, heavy, held_as=jnp.bfloat16):
    result = width * jax.random.normal(key, extent, jnp.float32)
    if shards:
        result = result * level_of(key, extent, shards, -0.22, 0.18)
    return jnp.clip(with_spikes(result, jax.random.fold_in(key, 3), *heavy), -reach, reach).astype(held_as)


def setup_inputs(seed: int = 0) -> dict:
    keys = jax.random.split(jax.random.key(seed), 16)
    return {
        "grad_a_parts": heavy_noise(keys[0], (GROUPS, POLICIES, D, R), 1.0, 6.0, ((0, 32), (2, 8)), (0, 1, 32, 2.75)),
        "grad_b_parts": heavy_noise(keys[1], (GROUPS, POLICIES, R, QD), 1.0, 6.0, ((0, 32), (3, 8)), (0, 1, 32, 2.75)),
        "adapter_a": noise(keys[2], (POLICIES, D, R), D ** -0.5, 0.078125, ((0, 32), (1, 8)), jnp.float32),
        "adapter_b": noise(keys[3], (POLICIES, R, QD), R ** -0.5, 0.75, ((0, 32), (2, 8)), jnp.float32),
        "moment_a": noise(keys[4], (POLICIES, D, R), 2.0, 8.0, ((0, 32), (1, 8)), jnp.float32),
        "moment_b": noise(keys[5], (POLICIES, R, QD), 2.0, 8.0, ((0, 32), (2, 8)), jnp.float32),
        "second_a": jnp.clip(jnp.exp(math.log(0.1) - 4.6051702 * jax.random.uniform(keys[6], (POLICIES, D, R), jnp.float32) ** level_of(keys[6], (POLICIES, D, R), ((0, 32), (1, 8)), -0.2, 0.2)), 0.001, 0.1),
        "second_b": jnp.clip(jnp.exp(math.log(0.1) - 4.6051702 * jax.random.uniform(keys[7], (POLICIES, R, QD), jnp.float32) ** level_of(keys[7], (POLICIES, R, QD), ((0, 32), (2, 8)), -0.2, 0.2)), 0.001, 0.1),
        "group_policy": draw_group_policy(jax.random.fold_in(keys[15], 71), 0),
        "row_slot": draw_row_slot(jax.random.fold_in(keys[15], 71), 0),
        "cache_length": draw_cache_length(jax.random.fold_in(keys[15], 71), 0),
        "features": noise(keys[11], (ROWS, D), 1.0, 6.0, ((0, 32), (1, 8))),
        "frozen_query_output": draw_frozen_query_output(jax.random.fold_in(keys[15], 71), 0),
        "kv_cache": draw_kv_cache(jax.random.fold_in(keys[15], 71), 0),
        "new_kv": draw_new_kv(jax.random.fold_in(keys[15], 71), 0),
    }


BETA_ONE = 0.9
BETA_TWO = 0.999
LEARN_RATE = 0.001
EPSILON = 1e-08
WEIGHT_SHRINKAGE = 0.01
LOWRANK_SCALE = 2.0
FIRST_FIX = 1.0 - 0.9 ** 10
SECOND_FIX = 1.0 - 0.999 ** 10

def adamw(param, moment, second, gradient):
    new_moment = BETA_ONE * moment + (1.0 - BETA_ONE) * gradient
    new_second = BETA_TWO * second + (1.0 - BETA_TWO) * gradient * gradient
    stepped = new_moment / FIRST_FIX / (jnp.sqrt(new_second / SECOND_FIX) + EPSILON)
    return (param - LEARN_RATE * (stepped + WEIGHT_SHRINKAGE * param), new_moment, new_second)

def summed(parts):

    def add_one(index, accum):
        return accum + parts[index].astype(jnp.float32)
    return lax.fori_loop(0, parts.shape[0], add_one, jnp.zeros(parts.shape[1:], jnp.float32))

def attend(query_vector, cache_keys, cache_values, new_key, new_value, length):
    count = query_vector.shape[0]
    kv_count = cache_keys.shape[1]
    head_width = cache_keys.shape[3]
    span = cache_keys.shape[2]
    inverse = 1.0 / math.sqrt(head_width)
    query_f = query_vector.reshape(count, kv_count, -1, head_width).astype(jnp.float32)
    scores = jnp.einsum('rkgd,rkcd->rkgc', query_f, cache_keys.astype(jnp.float32)) * inverse
    valid = (jnp.arange(span)[None, :] < length[:, None])[:, None, None, :]
    scores = jnp.where(valid, scores, -1e+30)
    own = jnp.einsum('rkgd,rkd->rkg', query_f, new_key.astype(jnp.float32)) * inverse
    peak = jnp.maximum(lax.optimization_barrier(jnp.max(scores, axis=-1)), own)
    weights = jnp.where(valid, jnp.exp(scores - peak[..., None]), 0.0)
    own_weight = jnp.exp(own - peak)
    denominator = lax.optimization_barrier(jnp.sum(weights, axis=-1)) + own_weight
    probs = (weights / denominator[..., None]).astype(jnp.bfloat16)
    own_prob = (own_weight / denominator).astype(jnp.bfloat16)
    mixed = jnp.einsum('rkgc,rkcd->rkgd', probs.astype(jnp.float32), cache_values.astype(jnp.float32))
    mixed = mixed + own_prob.astype(jnp.float32)[..., None] * new_value.astype(jnp.float32)[:, :, None, :]
    return mixed.reshape(count, -1).astype(jnp.bfloat16)

def reference(grad_a_parts, grad_b_parts, adapter_a, adapter_b, moment_a, moment_b, second_a, second_b, group_policy, row_slot, cache_length, features, frozen_query_output, kv_cache, new_kv):
    new_a, new_moment_a, new_second_a = adamw(adapter_a, moment_a, second_a, summed(grad_a_parts))
    new_b, new_moment_b, new_second_b = adamw(adapter_b, moment_b, second_b, summed(grad_b_parts))
    page_a = new_a.astype(jnp.bfloat16)
    page_b = new_b.astype(jnp.bfloat16)
    group_of_row = (jnp.arange(ROWS) // ROW_DEV).astype(jnp.int32)
    row_policy = group_policy[group_of_row, row_slot]

    def one_group(items):
        feats, frozen_base, cache_keys, cache_values, new_key, new_value, length, policy = items
        shrink = jnp.einsum('rd,rdk->rk', feats.astype(jnp.float32), page_a[policy].astype(jnp.float32))
        shrink = shrink.astype(jnp.bfloat16)
        enlarged_buffer = jnp.einsum('rk,rkn->rn', shrink.astype(jnp.float32), page_b[policy].astype(jnp.float32))
        query_vector = (frozen_base.astype(jnp.float32) + LOWRANK_SCALE * enlarged_buffer).astype(jnp.bfloat16)
        return attend(query_vector, cache_keys, cache_values, new_key, new_value, length)
    items = (features.reshape(GROUPS, ROW_DEV, D), frozen_query_output.reshape(GROUPS, ROW_DEV, QD), kv_cache[0].reshape(GROUPS, ROW_DEV, KVH, CACHE, HD), kv_cache[1].reshape(GROUPS, ROW_DEV, KVH, CACHE, HD), new_kv[0].reshape(GROUPS, ROW_DEV, KVH, HD), new_kv[1].reshape(GROUPS, ROW_DEV, KVH, HD), cache_length.reshape(GROUPS, ROW_DEV), row_policy.reshape(GROUPS, ROW_DEV))
    attended = lax.map(one_group, items).reshape(ROWS, QD)
    return (new_a, new_b, new_moment_a, new_moment_b, new_second_a, new_second_b, attended)
```

```python
import math

import jax
import jax.numpy as jnp
from jax import lax
from jax.sharding import Mesh
from jax.sharding import PartitionSpec as P

BETA_ONE = 0.9
BETA_TWO = 0.999
LEARN_RATE = 0.001
EPSILON = 1e-08
WEIGHT_SHRINKAGE = 0.01
LOWRANK_SCALE = 2.0
FIRST_FIX = 1.0 - 0.9**10
SECOND_FIX = 1.0 - 0.999**10
NZ, NY, NX, NC = 8, 4, 4, 2
SIZES = {"z": NZ, "y": NY, "x": NX, "c": NC}
F32 = jnp.float32
BF16 = jnp.bfloat16


def adamw(param, moment, second, gradient):
    new_moment = BETA_ONE * moment + (1.0 - BETA_ONE) * gradient
    new_second = BETA_TWO * second + (1.0 - BETA_TWO) * gradient * gradient
    stepped = new_moment / FIRST_FIX / (jnp.sqrt(new_second / SECOND_FIX) + EPSILON)
    return (param - LEARN_RATE * (stepped + WEIGHT_SHRINKAGE * param), new_moment, new_second)


def shift(value, axis, by):
    size = SIZES[axis]
    return lax.ppermute(value, axis, [(i, (i + by) % size) for i in range(size)])


def ring_sum(parts, axis, dim):
    size = SIZES[axis]
    me = lax.axis_index(axis)
    far = size // 2

    def chunk(offset):
        return lax.dynamic_index_in_dim(parts, lax.rem(me + (offset + size), size), dim, keepdims=False)

    first = chunk(far)
    half = first.shape[0] // 2
    low, high = first[:half], first[half:]
    spare = [(0, 0, 0)] * (first.ndim - 1)
    up, down = shift(high, axis, 1), shift(low, axis, -1)
    for step in range(1, far):
        up, down = up.astype(F32), down.astype(F32)
        if step == 1:
            zero = jnp.zeros((), F32)
            up = lax.pad(up, zero, [(half, 0, 0)] + spare)
            down = lax.pad(down, zero, [(0, half, 0)] + spare)
        up = (chunk(far - step).astype(F32) + up).astype(BF16)
        down = (chunk(step - far).astype(F32) + down).astype(BF16)
        up, down = shift(up, axis, 1), shift(down, axis, -1)
    return chunk(0).astype(F32) + up.astype(F32) + down.astype(F32)


def ring_gather(page):
    up = down = page
    pages = [page]
    for _ in range(3):
        up, down = shift(up, "z", 1), shift(down, "z", -1)
        pages += [up, down]
    half = page.shape[0] // 2
    low, high = shift(up[:half], "z", 1), shift(down[half:], "z", -1)
    pages.append(jnp.concatenate([low, high], axis=0))
    return pages


OFFSETS = (0, -1, 1, -2, 2, -3, 3, 4)


def tensor_sum(value):
    core = lax.axis_index("c")
    half = value.shape[0] // 2
    both = value.reshape(2, half, value.shape[1])
    mine = lax.dynamic_index_in_dim(both, core, 0, keepdims=False)
    other = lax.dynamic_index_in_dim(both, 1 - core, 0, keepdims=False)
    mine = mine + shift(other, "c", 1)
    total = (mine + shift(mine, "x", 2)) + (shift(mine, "x", 1) + shift(mine, "x", -1))
    total = total.astype(BF16)
    other = shift(total, "c", 1)
    return jnp.where(
        core == 0, jnp.concatenate([total, other], axis=0), jnp.concatenate([other, total], axis=0)
    )


def attend(query_vector, cache_keys, cache_values, new_key, new_value, length):
    count = query_vector.shape[0]
    kv_count = cache_keys.shape[1]
    head_width = cache_keys.shape[3]
    span = cache_keys.shape[2]
    inverse = 1.0 / math.sqrt(head_width)
    query_heads = query_vector.reshape(count, kv_count, -1, head_width)
    scores = (
        jnp.einsum("rkgd,rkcd->rkgc", query_heads, cache_keys, preferred_element_type=F32)
        * inverse
    )
    valid = (jnp.arange(span)[None, :] < length[:, None])[:, None, None, :]
    scores = jnp.where(valid, scores, -1e30)
    own = jnp.einsum("rkgd,rkd->rkg", query_heads, new_key, preferred_element_type=F32) * inverse
    peak = jnp.maximum(jnp.max(scores, axis=-1), own)
    weights = jnp.where(valid, jnp.exp(scores - peak[..., None]), 0.0)
    own_weight = jnp.exp(own - peak)
    denominator = jnp.sum(weights, axis=-1) + own_weight
    probs = (weights / denominator[..., None]).astype(BF16)
    own_prob = (own_weight / denominator).astype(BF16)
    mixed = jnp.einsum("rkgc,rkcd->rkgd", probs, cache_values, preferred_element_type=F32)
    mixed = mixed + own_prob.astype(F32)[..., None] * new_value.astype(F32)[:, :, None, :]
    return mixed.reshape(count, -1).astype(BF16)


def shards(
    grad_a_parts,
    grad_b_parts,
    adapter_a,
    adapter_b,
    moment_a,
    moment_b,
    second_a,
    second_b,
    group_policy,
    row_slot,
    cache_length,
    features,
    frozen_query_output,
    kv_cache,
    new_kv,
):
    z, y = lax.axis_index("z"), lax.axis_index("y")
    rows, width = features.shape
    rank = grad_b_parts.shape[2]
    flip = lambda value: jnp.swapaxes(value, -1, -2)

    my_policies = lax.dynamic_index_in_dim(group_policy, z * NY + y, 0, keepdims=False)
    slot_onehot = row_slot[:, None] == jnp.arange(my_policies.shape[0])[None, :]
    row_policy = jnp.sum(jnp.where(slot_onehot, my_policies[None, :], 0), axis=1)
    label = lax.pad(
        row_policy.astype(BF16)[None, :], jnp.zeros((), BF16), [(0, 15, 0), (0, width - rows, 0)]
    )
    packed = jnp.concatenate([features, label], axis=0)

    parts_a = flip(grad_a_parts[0]).reshape(NZ, NY, rank, width)
    parts_b = grad_b_parts[0].reshape(NZ, NY, rank, grad_b_parts.shape[3])

    sum_a = ring_sum(parts_a, "z", 0)
    sum_b = ring_sum(parts_b, "y", 1)
    grad_a = ring_sum(sum_a.astype(BF16), "y", 0)
    grad_b = ring_sum(sum_b.astype(BF16), "z", 0)
    new_a, new_moment_a, new_second_a = adamw(
        flip(adapter_a[0]), flip(moment_a[0]), flip(second_a[0]), grad_a
    )
    new_b, new_moment_b, new_second_b = adamw(adapter_b[0], moment_b[0], second_b[0], grad_b)

    packs = [packed] + [shift(packed, "y", -by) for by in (1, 2, 3)]
    feats = jnp.concatenate([pack[:rows] for pack in packs], axis=0)
    policies = jnp.concatenate([pack[rows, :rows] for pack in packs], axis=0).astype(jnp.int32)
    owned = jnp.stack([lax.rem(z + (by + NZ), NZ) * NY + y for by in OFFSETS])
    chosen = owned[:, None] == policies[None, :]

    pages_a = jnp.stack(ring_gather(new_a.astype(BF16)))
    projected = jnp.einsum("pkd,rd->pkr", pages_a, feats, preferred_element_type=F32)
    partial = jnp.sum(jnp.where(chosen[:, None, :], projected, 0.0), axis=0)
    shrink = tensor_sum(partial)

    pages_b = jnp.stack(ring_gather(new_b.astype(BF16)))
    spread = jnp.where(chosen[:, None, :], shrink[None], jnp.zeros((), BF16))
    delta = jnp.einsum("pkr,pkn->rn", spread, pages_b, preferred_element_type=F32).astype(BF16)

    delta = delta.reshape(NY, rows, -1)
    mine = (
        (delta[0].astype(F32) + shift(delta[2], "y", 2).astype(F32))
        + (shift(delta[1], "y", 1).astype(F32) + shift(delta[3], "y", 3).astype(F32))
    )
    query_vector = (frozen_query_output.astype(F32) + LOWRANK_SCALE * mine).astype(BF16)
    attended = attend(query_vector, kv_cache[0], kv_cache[1], new_kv[0], new_kv[1], cache_length)
    return (
        flip(new_a)[None],
        new_b[None],
        flip(new_moment_a)[None],
        new_moment_b[None],
        flip(new_second_a)[None],
        new_second_b[None],
        attended,
    )


def solution(mesh):
    fine = Mesh(mesh.devices.reshape(NZ, NY, NX, NC), ("z", "y", "x", "c"))
    dp, tensor = ("z", "y"), ("x", "c")
    adapter_a, adapter_b = P(dp, tensor, None), P(dp, None, tensor)
    return jax.shard_map(
        shards,
        mesh=fine,
        in_specs=(
            P(dp, None, tensor, None),
            P(dp, None, None, tensor),
            adapter_a,
            adapter_b,
            adapter_a,
            adapter_b,
            adapter_a,
            adapter_b,
            P(),
            P(dp),
            P(dp),
            P(dp, tensor),
            P(dp, tensor),
            P(None, dp, tensor, None, None),
            P(None, dp, tensor, None),
        ),
        out_specs=(adapter_a, adapter_b, adapter_a, adapter_b, adapter_a, adapter_b, P(dp, tensor)),
        check_vma=False,
    )
```

```python
import math

import jax
import jax.numpy as jnp
from jax import lax
from jax.experimental import pallas as pl
from jax.experimental.pallas import tpu as pltpu
from jax.sharding import Mesh
from jax.sharding import PartitionSpec as P

BETA_ONE = 0.9
BETA_TWO = 0.999
LEARN_RATE = 0.001
EPSILON = 1e-08
WEIGHT_SHRINKAGE = 0.01
LOWRANK_SCALE = 2.0
FIRST_FIX = 1.0 - 0.9**10
SECOND_FIX = 1.0 - 0.999**10
NZ, NY, NX, NC = 8, 4, 4, 2
SIZES = {"z": NZ, "y": NY, "x": NX, "c": NC}
F32 = jnp.float32
BF16 = jnp.bfloat16
CAP = 16
PIECES = 2


def adamw(param, moment, second, gradient):
    new_moment = BETA_ONE * moment + (1.0 - BETA_ONE) * gradient
    new_second = BETA_TWO * second + (1.0 - BETA_TWO) * gradient * gradient
    stepped = new_moment / FIRST_FIX / (jnp.sqrt(new_second / SECOND_FIX) + EPSILON)
    return (param - LEARN_RATE * (stepped + WEIGHT_SHRINKAGE * param), new_moment, new_second)


def shift(value, axis, by):
    size = SIZES[axis]
    return lax.ppermute(value, axis, [(i, (i + by) % size) for i in range(size)])


def crossed(value, by, flip):
    pairs = [(2 * x + c, 2 * ((x + by) % NX) + (c ^ flip)) for x in range(NX) for c in range(NC)]
    return lax.ppermute(value, ("x", "c"), pairs)


def tied(*values):
    return lax.optimization_barrier(values)


def after(values, *done):
    return lax.optimization_barrier((*values, *done))[: len(values)]


class Ring:
    def __init__(self, parts, axis, dim):
        self.parts, self.axis, self.dim = parts, axis, dim
        self.size, self.me = SIZES[axis], lax.axis_index(axis)
        self.left = self.size // 2

    def chunk(self, offset):
        place = lax.rem(self.me + (offset + self.size), self.size)
        return lax.dynamic_index_in_dim(self.parts, place, self.dim, keepdims=False)

    def send(self, up, down):
        up, down = tied(up, down)
        return tied(shift(up, self.axis, 1), shift(down, self.axis, -1))

    def first(self):
        chunk = self.chunk(self.left)
        self.half = chunk.shape[0] // 2
        return chunk[self.half :], chunk[: self.half]

    def step(self, up, down):
        up, down = up.astype(F32), down.astype(F32)
        if 2 * self.left == self.size:
            spare = [(0, 0, 0)] * (up.ndim - 1)
            zero = jnp.zeros((), F32)
            up = lax.pad(up, zero, [(self.half, 0, 0)] + spare)
            down = lax.pad(down, zero, [(0, self.half, 0)] + spare)
        self.left -= 1
        up = (self.chunk(self.left).astype(F32) + up).astype(BF16)
        down = (self.chunk(-self.left).astype(F32) + down).astype(BF16)
        return up, down

    def total(self, up, down):
        return (self.chunk(0).astype(F32) + up.astype(F32) + down.astype(F32)).astype(BF16)


def swapped_sum(parts, axis):
    parts = lax.all_to_all(parts, axis, 0, 0)
    terms = [parts[i].astype(F32) for i in range(SIZES[axis])]
    while len(terms) > 1:
        terms = [left + right for left, right in zip(terms[::2], terms[1::2])]
    return terms[0]


def sent_sum(parts, axis):
    size = SIZES[axis]
    me = lax.axis_index(axis)

    def chunk(offset):
        return lax.dynamic_index_in_dim(parts, lax.rem(me + offset, size), 0, keepdims=False)

    sent = tied(*[chunk(offset) for offset in range(1, size)])
    came = tied(*[shift(part, axis, 1 + i) for i, part in enumerate(sent)])
    total = chunk(0).astype(F32)
    for part in came:
        total = total + part.astype(F32)
    return total, sent


def tensor_sum(value):
    core = lax.axis_index("c")
    both = (value + shift(value, "c", 1)).reshape(2, value.shape[0] // 2, value.shape[1])
    mine = lax.dynamic_index_in_dim(both, core, 0, keepdims=False)
    other = lax.dynamic_index_in_dim(both, 1 - core, 0, keepdims=False)
    mine, other = tied(mine, other)
    one, two, three = tied(crossed(other, 1, 1), crossed(mine, NX - 1, 0), crossed(mine, 2, 0))
    total = ((mine + one) + (two + three)).astype(BF16)
    other = shift(total, "c", 1)
    return jnp.where(
        core == 0, jnp.concatenate([total, other], axis=0), jnp.concatenate([other, total], axis=0)
    )


def decode_kernel(place_ref, length_ref, delta_ref, frozen_ref, cache_hbm, new_ref, out_ref, query, cache_ref, arrived):
    block = out_ref.shape[0] // PIECES
    copies = []
    for piece in range(PIECES):
        part = (slice(None), slice(piece * block, (piece + 1) * block))
        copies.append(pltpu.make_async_copy(cache_hbm.at[part], cache_ref.at[part], arrived.at[piece]))
        copies[-1].start()
    total, spots = query.shape[0], delta_ref.shape[0]
    pick = lax.broadcasted_iota(jnp.int32, (total, spots), 1) == place_ref[...]
    pick = jnp.where(pick, 1.0, 0.0).astype(BF16)
    mine = jnp.dot(pick, delta_ref[...], preferred_element_type=F32)
    vector = frozen_ref[...].astype(F32) + LOWRANK_SCALE * mine
    query[...] = vector.astype(BF16).astype(F32)
    for piece in range(PIECES):
        copies[piece].wait()
        decode_rows(piece * block, block, length_ref, cache_ref, new_ref, out_ref, query)


def decode_rows(base, block, length_ref, cache_ref, new_ref, out_ref, query):
    span, width = cache_ref.shape[3], cache_ref.shape[4]
    heads = out_ref.shape[1] // width
    inverse = 1.0 / math.sqrt(width)
    column = lax.broadcasted_iota(jnp.int32, (8, 8 * span), 1)
    first = lax.broadcasted_iota(jnp.int32, (8, 8 * span), 0) * span
    starts = range(base, base + block, 8)
    stack = lambda value: jnp.concatenate([value] * heads, axis=0)
    rows, scores, valid = [], [], []
    for low in starts:
        piece = query[low : low + 8, :]
        piece = jnp.concatenate([piece[:, h * width : (h + 1) * width] for h in range(heads)], axis=0)
        keys = cache_ref[0, low : low + 8, 0].reshape(8 * span, width)
        rows.append(piece)
        scores.append(
            lax.dot_general(piece.astype(BF16), keys, (((1,), (1,)), ((), ())), preferred_element_type=F32)
        )
    probs, own_probs = [], []
    for i, low in enumerate(starts):
        length = length_ref[low : low + 8, :]
        valid = (column >= first) & (column < first + length)
        bias = stack(jnp.where(valid, 0.0, -1e30))
        score = scores[i] * inverse + bias
        own = jnp.sum(rows[i] * stack(new_ref[0, low : low + 8, :].astype(F32)), axis=1, keepdims=True) * inverse
        peak = jnp.maximum(jnp.max(score, axis=1, keepdims=True), own)
        weights = jnp.exp(score - peak)
        own_weight = jnp.exp(own - peak)
        scale = 1.0 / (jnp.sum(weights, axis=1, keepdims=True) + own_weight)
        probs.append((weights * scale).astype(BF16))
        own_probs.append((own_weight * scale).astype(BF16).astype(F32))
    mixed = []
    for i, low in enumerate(starts):
        values = cache_ref[1, low : low + 8, 0].reshape(8 * span, width)
        new_value = stack(new_ref[1, low : low + 8, :].astype(F32))
        mixed.append(jnp.dot(probs[i], values, preferred_element_type=F32) + own_probs[i] * new_value)
    for h in range(heads):
        part = jnp.concatenate([value[8 * h : 8 * h + 8] for value in mixed], axis=0)
        out_ref[base : base + block, h * width : (h + 1) * width] = part.astype(BF16)


def decode(place, length, delta, frozen, kv_cache, new_kv):
    vmem = pl.BlockSpec(memory_space=pltpu.VMEM)
    return pl.pallas_call(
        decode_kernel,
        in_specs=[vmem] * 4 + [pl.BlockSpec(memory_space=pltpu.HBM), vmem],
        out_specs=vmem,
        out_shape=jax.ShapeDtypeStruct(frozen.shape, BF16),
        scratch_shapes=[
            pltpu.VMEM(frozen.shape, F32),
            pltpu.VMEM(kv_cache.shape, BF16),
            pltpu.SemaphoreType.DMA((PIECES,)),
        ],
        compiler_params=pltpu.CompilerParams(vmem_limit_bytes=32 * 1024 * 1024),
    )(place[:, None], length[:, None], delta, frozen, kv_cache, new_kv[:, :, 0])


def shards(
    grad_a_parts,
    grad_b_parts,
    adapter_a,
    adapter_b,
    moment_a,
    moment_b,
    second_a,
    second_b,
    group_policy,
    row_slot,
    cache_length,
    features,
    frozen_query_output,
    kv_cache,
    new_kv,
):
    z, y = lax.axis_index("z"), lax.axis_index("y")
    rows, width = features.shape
    rank = grad_b_parts.shape[2]
    policies = group_policy.shape[0]
    flip = lambda value: jnp.swapaxes(value, -1, -2)

    ring_a = Ring(flip(grad_a_parts[0]).reshape(NZ, NY, rank, width), "z", 0)
    ring_b = Ring(grad_b_parts[0].reshape(NZ, NY, rank, grad_b_parts.shape[3]), "y", 1)
    go_a = ring_a.first()
    go_b = after(ring_b.first(), *go_a)
    come_a, come_b = ring_a.send(*go_a), ring_b.send(*go_b)
    (row_slot,) = after((row_slot,), *go_b)

    my_policies = lax.dynamic_index_in_dim(group_policy, z * NY + y, 0, keepdims=False)
    slot_onehot = row_slot[:, None] == jnp.arange(my_policies.shape[0])[None, :]
    row_policy = jnp.sum(jnp.where(slot_onehot, my_policies[None, :], 0), axis=1)
    before = jnp.sum((row_slot[None, :] < row_slot[:, None]).astype(jnp.int32), axis=1)
    place = row_policy * CAP + jnp.arange(rows, dtype=jnp.int32) - before
    select = (jnp.arange(policies * CAP, dtype=jnp.int32)[:, None] == place[None, :]).astype(BF16)

    packed = jnp.dot(select, features, preferred_element_type=F32).astype(BF16)

    come_a = after(come_a, packed)
    go_a = ring_a.step(*come_a)
    come_a = ring_a.send(*go_a)
    (packed,) = after((packed,), *go_a)
    feats = lax.all_to_all(packed.reshape(policies, CAP, width), ("z", "y"), 0, 0)
    go_b = ring_b.step(*after(come_b, packed))
    come_b = ring_b.send(*go_b)
    go_a = ring_a.step(*after(come_a, *go_b))
    come_a = ring_a.send(*go_a)
    *come_a, feats = tied(*come_a, feats)
    go_a = ring_a.step(*come_a)
    come_a = ring_a.send(*go_a)
    sum_b = ring_b.total(*after(come_b, *go_a))
    grad_b = swapped_sum(sum_b, "z")
    grad_a, _ = sent_sum(ring_a.total(*after(come_a, sum_b)), "y")
    feats = feats.reshape(policies * CAP, width)

    new_a, new_moment_a, new_second_a = adamw(
        flip(adapter_a[0]), flip(moment_a[0]), flip(second_a[0]), grad_a
    )
    partial = lax.dot_general(
        new_a.astype(BF16), feats, (((1,), (1,)), ((), ())), preferred_element_type=F32
    )
    shrink = tensor_sum(partial)

    new_b, new_moment_b, new_second_b = adamw(adapter_b[0], moment_b[0], second_b[0], grad_b)
    delta = lax.dot_general(
        shrink, new_b.astype(BF16), (((0,), (0,)), ((), ())), preferred_element_type=F32
    ).astype(BF16)
    delta = lax.all_to_all(delta.reshape(policies, CAP, -1), ("z", "y"), 0, 0)
    delta = delta.reshape(policies * CAP, -1)
    attended = decode(place, cache_length, delta, frozen_query_output, kv_cache, new_kv)
    return (
        flip(new_a)[None],
        new_b[None],
        flip(new_moment_a)[None],
        new_moment_b[None],
        flip(new_second_a)[None],
        new_second_b[None],
        attended,
    )


def solution(mesh):
    fine = Mesh(mesh.devices.reshape(NZ, NY, NX, NC), ("z", "y", "x", "c"))
    dp, tensor = ("z", "y"), ("x", "c")
    adapter_a, adapter_b = P(dp, tensor, None), P(dp, None, tensor)
    return jax.shard_map(
        shards,
        mesh=fine,
        in_specs=(
            P(dp, None, tensor, None),
            P(dp, None, None, tensor),
            adapter_a,
            adapter_b,
            adapter_a,
            adapter_b,
            adapter_a,
            adapter_b,
            P(),
            P(dp),
            P(dp),
            P(dp, tensor),
            P(dp, tensor),
            P(None, dp, tensor, None, None),
            P(None, dp, tensor, None),
        ),
        out_specs=(adapter_a, adapter_b, adapter_a, adapter_b, adapter_a, adapter_b, P(dp, tensor)),
        check_vma=False,
    )
```

```python
import math

import jax
import jax.numpy as jnp
from jax import lax
from jax.experimental import pallas as pl
from jax.experimental.pallas import tpu as pltpu
from jax.sharding import Mesh
from jax.sharding import PartitionSpec as P

BETA_ONE = 0.9
BETA_TWO = 0.999
LEARN_RATE = 0.001
EPSILON = 1e-08
WEIGHT_SHRINKAGE = 0.01
LOWRANK_SCALE = 2.0
FIRST_FIX = 1.0 - 0.9**10
SECOND_FIX = 1.0 - 0.999**10
NZ, NY, NX, NC = 8, 4, 4, 2
SIZES = {"z": NZ, "y": NY, "x": NX, "c": NC}
F32 = jnp.float32
BF16 = jnp.bfloat16
CAP = 16
PIECES = 2


def adamw(param, moment, second, gradient):
    new_moment = BETA_ONE * moment + (1.0 - BETA_ONE) * gradient
    new_second = BETA_TWO * second + (1.0 - BETA_TWO) * gradient * gradient
    stepped = new_moment / FIRST_FIX / (jnp.sqrt(new_second / SECOND_FIX) + EPSILON)
    return (param - LEARN_RATE * (stepped + WEIGHT_SHRINKAGE * param), new_moment, new_second)


def shift(value, axis, by):
    size = SIZES[axis]
    return lax.ppermute(value, axis, [(i, (i + by) % size) for i in range(size)])


def crossed(value, by, flip):
    pairs = [(2 * x + c, 2 * ((x + by) % NX) + (c ^ flip)) for x in range(NX) for c in range(NC)]
    return lax.ppermute(value, ("x", "c"), pairs)


def tied(*values):
    return lax.optimization_barrier(values)


def after(values, *done):
    return lax.optimization_barrier((*values, *done))[: len(values)]


class Ring:
    def __init__(self, parts, axis, dim):
        self.parts, self.axis, self.dim = parts, axis, dim
        self.size, self.me = SIZES[axis], lax.axis_index(axis)
        self.left = self.size // 2

    def chunk(self, offset):
        place = lax.rem(self.me + (offset + self.size), self.size)
        return lax.dynamic_index_in_dim(self.parts, place, self.dim, keepdims=False)

    def send(self, up, down):
        up, down = tied(up, down)
        return tied(shift(up, self.axis, 1), shift(down, self.axis, -1))

    def first(self):
        chunk = self.chunk(self.left)
        self.half = chunk.shape[0] // 2
        return chunk[self.half :], chunk[: self.half]

    def step(self, up, down):
        up, down = up.astype(F32), down.astype(F32)
        if 2 * self.left == self.size:
            spare = [(0, 0, 0)] * (up.ndim - 1)
            zero = jnp.zeros((), F32)
            up = lax.pad(up, zero, [(self.half, 0, 0)] + spare)
            down = lax.pad(down, zero, [(0, self.half, 0)] + spare)
        self.left -= 1
        up = (self.chunk(self.left).astype(F32) + up).astype(BF16)
        down = (self.chunk(-self.left).astype(F32) + down).astype(BF16)
        return up, down

    def total(self, up, down):
        return (self.chunk(0).astype(F32) + up.astype(F32) + down.astype(F32)).astype(BF16)


def swapped_sum(parts, axis):
    parts = lax.all_to_all(parts, axis, 0, 0)
    terms = [parts[i].astype(F32) for i in range(SIZES[axis])]
    while len(terms) > 1:
        terms = [left + right for left, right in zip(terms[::2], terms[1::2])]
    return terms[0]


def sent_sum(parts, axis):
    size = SIZES[axis]
    me = lax.axis_index(axis)

    def chunk(offset):
        return lax.dynamic_index_in_dim(parts, lax.rem(me + offset, size), 0, keepdims=False)

    sent = tied(*[chunk(offset) for offset in range(1, size)])
    came = tied(*[shift(part, axis, 1 + i) for i, part in enumerate(sent)])
    total = chunk(0).astype(F32)
    for part in came:
        total = total + part.astype(F32)
    return total, sent


def tensor_sum(value, state):
    core = lax.axis_index("c")
    both = (value + shift(value, "c", 1)).reshape(2, value.shape[0] // 2, value.shape[1])
    mine = lax.dynamic_index_in_dim(both, core, 0, keepdims=False)
    other = lax.dynamic_index_in_dim(both, 1 - core, 0, keepdims=False)
    mine, other = tied(mine, other)
    one, two, three = tied(crossed(other, 1, 1), crossed(mine, NX - 1, 0), crossed(mine, 2, 0))
    new = adamw(*after(state, mine))
    one, two, three = after((one, two, three), *new)
    total = ((mine + one) + (two + three)).astype(BF16)
    other = shift(total, "c", 1)
    total = jnp.where(
        core == 0, jnp.concatenate([total, other], axis=0), jnp.concatenate([other, total], axis=0)
    )
    return total, *new


def decode_kernel(place_ref, length_ref, delta_ref, frozen_ref, cache_hbm, new_ref, out_ref, query, cache_ref, arrived):
    block = out_ref.shape[0] // PIECES
    copies = []
    for piece in range(PIECES):
        part = (slice(None), slice(piece * block, (piece + 1) * block))
        copies.append(pltpu.make_async_copy(cache_hbm.at[part], cache_ref.at[part], arrived.at[piece]))
        copies[-1].start()
    total, spots = query.shape[0], delta_ref.shape[0]
    pick = lax.broadcasted_iota(jnp.int32, (total, spots), 1) == place_ref[...]
    pick = jnp.where(pick, 1.0, 0.0).astype(BF16)
    mine = jnp.dot(pick, delta_ref[...], preferred_element_type=F32)
    vector = frozen_ref[...].astype(F32) + LOWRANK_SCALE * mine
    query[...] = vector.astype(BF16).astype(F32)
    for piece in range(PIECES):
        copies[piece].wait()
        decode_rows(piece * block, block, length_ref, cache_ref, new_ref, out_ref, query)


def decode_rows(base, block, length_ref, cache_ref, new_ref, out_ref, query):
    span, width = cache_ref.shape[3], cache_ref.shape[4]
    heads = out_ref.shape[1] // width
    inverse = 1.0 / math.sqrt(width)
    column = lax.broadcasted_iota(jnp.int32, (8, 8 * span), 1)
    first = lax.broadcasted_iota(jnp.int32, (8, 8 * span), 0) * span
    starts = range(base, base + block, 8)
    new = new_ref[:, base : base + block, :].astype(F32)
    stack = lambda value: jnp.concatenate([value] * heads, axis=0)
    rows, scores, valid = [], [], []
    for low in starts:
        piece = query[low : low + 8, :]
        piece = jnp.concatenate([piece[:, h * width : (h + 1) * width] for h in range(heads)], axis=0)
        keys = cache_ref[0, low : low + 8, 0].reshape(8 * span, width)
        rows.append(piece)
        scores.append(
            lax.dot_general(piece.astype(BF16), keys, (((1,), (1,)), ((), ())), preferred_element_type=F32)
        )
    probs, own_probs = [], []
    for i, low in enumerate(starts):
        length = length_ref[low : low + 8, :]
        valid = (column >= first) & (column < first + length)
        bias = stack(jnp.where(valid, 0.0, -1e30))
        score = scores[i] * inverse + bias
        own = jnp.sum(rows[i] * stack(new[0, 8 * i : 8 * i + 8]), axis=1, keepdims=True) * inverse
        peak = jnp.maximum(jnp.max(score, axis=1, keepdims=True), own)
        weights = jnp.exp(score - peak)
        own_weight = jnp.exp(own - peak)
        scale = 1.0 / (jnp.sum(weights, axis=1, keepdims=True) + own_weight)
        probs.append((weights * scale).astype(BF16))
        own_probs.append((own_weight * scale).astype(BF16).astype(F32))
    mixed = []
    for i, low in enumerate(starts):
        values = cache_ref[1, low : low + 8, 0].reshape(8 * span, width)
        new_value = stack(new[1, 8 * i : 8 * i + 8])
        mixed.append(jnp.dot(probs[i], values, preferred_element_type=F32) + own_probs[i] * new_value)
    for h in range(heads):
        part = jnp.concatenate([value[8 * h : 8 * h + 8] for value in mixed], axis=0)
        out_ref[base : base + block, h * width : (h + 1) * width] = part.astype(BF16)


def decode(place, length, delta, frozen, kv_cache, new_kv):
    vmem = pl.BlockSpec(memory_space=pltpu.VMEM)
    kv_cache = pltpu.with_memory_space_constraint(kv_cache, pltpu.HBM)
    return pl.pallas_call(
        decode_kernel,
        in_specs=[vmem] * 4 + [pl.BlockSpec(memory_space=pltpu.HBM), vmem],
        out_specs=vmem,
        out_shape=jax.ShapeDtypeStruct(frozen.shape, BF16),
        scratch_shapes=[
            pltpu.VMEM(frozen.shape, F32),
            pltpu.VMEM(kv_cache.shape, BF16),
            pltpu.SemaphoreType.DMA((PIECES,)),
        ],
        compiler_params=pltpu.CompilerParams(vmem_limit_bytes=32 * 1024 * 1024),
    )(place[:, None], length[:, None], delta, frozen, kv_cache, new_kv[:, :, 0])


def shards(
    grad_a_parts,
    grad_b_parts,
    adapter_a,
    adapter_b,
    moment_a,
    moment_b,
    second_a,
    second_b,
    group_policy,
    row_slot,
    cache_length,
    features,
    frozen_query_output,
    kv_cache,
    new_kv,
):
    z, y = lax.axis_index("z"), lax.axis_index("y")
    rows, width = features.shape
    rank = grad_b_parts.shape[2]
    policies = group_policy.shape[0]
    flip = lambda value: jnp.swapaxes(value, -1, -2)

    ring_a = Ring(flip(grad_a_parts[0]).reshape(NZ, NY, rank, width), "z", 0)
    ring_b = Ring(grad_b_parts[0].reshape(NZ, NY, rank, grad_b_parts.shape[3]), "y", 1)
    go_a = ring_a.first()
    go_b = after(ring_b.first(), *go_a)
    come_a, come_b = ring_a.send(*go_a), ring_b.send(*go_b)
    (row_slot,) = after((row_slot,), *go_b)

    my_policies = lax.dynamic_index_in_dim(group_policy, z * NY + y, 0, keepdims=False)
    slot_onehot = row_slot[:, None] == jnp.arange(my_policies.shape[0])[None, :]
    row_policy = jnp.sum(jnp.where(slot_onehot, my_policies[None, :], 0), axis=1)
    before = jnp.sum((row_slot[None, :] < row_slot[:, None]).astype(jnp.int32), axis=1)
    place = row_policy * CAP + jnp.arange(rows, dtype=jnp.int32) - before
    select = (jnp.arange(policies * CAP, dtype=jnp.int32)[:, None] == place[None, :]).astype(BF16)

    packed = jnp.dot(select, features, preferred_element_type=F32).astype(BF16)

    come_a = after(come_a, packed)
    go_a = ring_a.step(*come_a)
    come_a = ring_a.send(*go_a)
    (packed,) = after((packed,), *go_a)
    feats = lax.all_to_all(packed.reshape(policies, CAP, width), ("z", "y"), 0, 0)
    go_b = ring_b.step(*after(come_b, packed))
    come_b = ring_b.send(*go_b)
    go_a = ring_a.step(*after(come_a, *go_b))
    come_a = ring_a.send(*go_a)
    *come_a, feats = tied(*come_a, feats)
    go_a = ring_a.step(*come_a)
    come_a = ring_a.send(*go_a)
    sum_b = ring_b.total(*after(come_b, *go_a))
    grad_b = swapped_sum(sum_b, "z")
    grad_a, _ = sent_sum(ring_a.total(*after(come_a, sum_b)), "y")
    feats = feats.reshape(policies * CAP, width)

    state_a = [flip(value[0]) for value in (adapter_a, moment_a, second_a)] + [grad_a]
    page_a = adamw(*state_a)[0].astype(BF16)
    partial = lax.dot_general(page_a, feats, (((1,), (1,)), ((), ())), preferred_element_type=F32)
    shrink, new_a, new_moment_a, new_second_a = tensor_sum(partial, state_a)

    state_b = [value[0] for value in (adapter_b, moment_b, second_b)] + [grad_b]
    page_b = adamw(*state_b)[0].astype(BF16)
    delta = lax.dot_general(
        shrink, page_b, (((0,), (0,)), ((), ())), preferred_element_type=F32
    ).astype(BF16)
    new_b, new_moment_b, new_second_b = adamw(*after(state_b, delta))
    delta = lax.all_to_all(delta.reshape(policies, CAP, -1), ("z", "y"), 0, 0)
    delta = delta.reshape(policies * CAP, -1)
    attended = decode(place, cache_length, delta, frozen_query_output, kv_cache, new_kv)
    return (
        flip(new_a)[None],
        new_b[None],
        flip(new_moment_a)[None],
        new_moment_b[None],
        flip(new_second_a)[None],
        new_second_b[None],
        attended,
    )


def solution(mesh):
    fine = Mesh(mesh.devices.reshape(NZ, NY, NX, NC), ("z", "y", "x", "c"))
    dp, tensor = ("z", "y"), ("x", "c")
    adapter_a, adapter_b = P(dp, tensor, None), P(dp, None, tensor)
    return jax.shard_map(
        shards,
        mesh=fine,
        in_specs=(
            P(dp, None, tensor, None),
            P(dp, None, None, tensor),
            adapter_a,
            adapter_b,
            adapter_a,
            adapter_b,
            adapter_a,
            adapter_b,
            P(),
            P(dp),
            P(dp),
            P(dp, tensor),
            P(dp, tensor),
            P(None, dp, tensor, None, None),
            P(None, dp, tensor, None),
        ),
        out_specs=(adapter_a, adapter_b, adapter_a, adapter_b, adapter_a, adapter_b, P(dp, tensor)),
        check_vma=False,
    )
```

```python
import math

import jax
import jax.numpy as jnp
from jax import lax
from jax.experimental import pallas as pl
from jax.experimental.pallas import tpu as pltpu
from jax.sharding import Mesh
from jax.sharding import PartitionSpec as P

BETA_ONE = 0.9
BETA_TWO = 0.999
LEARN_RATE = 0.001
EPSILON = 1e-08
WEIGHT_SHRINKAGE = 0.01
LOWRANK_SCALE = 2.0
FIRST_FIX = 1.0 - 0.9**10
SECOND_FIX = 1.0 - 0.999**10
NZ, NY, NX, NC = 8, 4, 4, 2
SIZES = {"z": NZ, "y": NY, "x": NX, "c": NC}
F32 = jnp.float32
BF16 = jnp.bfloat16
CAP = 16
PIECES = 2


def adamw(param, moment, second, gradient):
    new_moment = BETA_ONE * moment + (1.0 - BETA_ONE) * gradient
    new_second = BETA_TWO * second + (1.0 - BETA_TWO) * gradient * gradient
    stepped = new_moment / FIRST_FIX / (jnp.sqrt(new_second / SECOND_FIX) + EPSILON)
    return (param - LEARN_RATE * (stepped + WEIGHT_SHRINKAGE * param), new_moment, new_second)


def shift(value, axis, by):
    size = SIZES[axis]
    return lax.ppermute(value, axis, [(i, (i + by) % size) for i in range(size)])


def crossed(value, by, flip):
    pairs = [(2 * x + c, 2 * ((x + by) % NX) + (c ^ flip)) for x in range(NX) for c in range(NC)]
    return lax.ppermute(value, ("x", "c"), pairs)


def tied(*values):
    return lax.optimization_barrier(values)


def after(values, *done):
    return lax.optimization_barrier((*values, *done))[: len(values)]


class Ring:
    def __init__(self, parts, axis, dim):
        self.parts, self.axis, self.dim = parts, axis, dim
        self.size, self.me = SIZES[axis], lax.axis_index(axis)
        self.left = self.size // 2

    def chunk(self, offset):
        place = lax.rem(self.me + (offset + self.size), self.size)
        return lax.dynamic_index_in_dim(self.parts, place, self.dim, keepdims=False)

    def send(self, up, down):
        up, down = tied(up, down)
        return tied(shift(up, self.axis, 1), shift(down, self.axis, -1))

    def first(self):
        chunk = self.chunk(self.left)
        self.half = chunk.shape[0] // 2
        return chunk[self.half :], chunk[: self.half]

    def step(self, up, down):
        up, down = up.astype(F32), down.astype(F32)
        if 2 * self.left == self.size:
            spare = [(0, 0, 0)] * (up.ndim - 1)
            zero = jnp.zeros((), F32)
            up = lax.pad(up, zero, [(self.half, 0, 0)] + spare)
            down = lax.pad(down, zero, [(0, self.half, 0)] + spare)
        self.left -= 1
        up = (self.chunk(self.left).astype(F32) + up).astype(BF16)
        down = (self.chunk(-self.left).astype(F32) + down).astype(BF16)
        return up, down

    def total(self, up, down):
        return (self.chunk(0).astype(F32) + up.astype(F32) + down.astype(F32)).astype(BF16)


def swapped_sum(parts, axis):
    parts = lax.all_to_all(parts, axis, 0, 0)
    terms = [parts[i].astype(F32) for i in range(SIZES[axis])]
    while len(terms) > 1:
        terms = [left + right for left, right in zip(terms[::2], terms[1::2])]
    return terms[0]


def sent_sum(parts, axis):
    size = SIZES[axis]
    me = lax.axis_index(axis)

    def chunk(offset):
        return lax.dynamic_index_in_dim(parts, lax.rem(me + offset, size), 0, keepdims=False)

    sent = tied(*[chunk(offset) for offset in range(1, size)])
    came = tied(*[shift(part, axis, 1 + i) for i, part in enumerate(sent)])
    total = chunk(0).astype(F32)
    for part in came:
        total = total + part.astype(F32)
    return total, sent


def tensor_sum(value, state):
    core = lax.axis_index("c")
    both = (value + shift(value, "c", 1)).reshape(2, value.shape[0] // 2, value.shape[1])
    mine = lax.dynamic_index_in_dim(both, core, 0, keepdims=False)
    other = lax.dynamic_index_in_dim(both, 1 - core, 0, keepdims=False)
    mine, other = tied(mine, other)
    sent, other = mine.astype(BF16), other.astype(BF16)
    one, two, three = tied(crossed(other, 1, 1), crossed(sent, NX - 1, 0), crossed(sent, 2, 0))
    new = adamw(*after(state, mine))
    one, two, three = [part.astype(F32) for part in after((one, two, three), *new)]
    total = ((mine + one) + (two + three)).astype(BF16)
    other = shift(total, "c", 1)
    total = jnp.where(
        core == 0, jnp.concatenate([total, other], axis=0), jnp.concatenate([other, total], axis=0)
    )
    return total, *new


def decode_kernel(place_ref, length_ref, delta_ref, frozen_ref, cache_hbm, new_ref, out_ref, query, cache_ref, arrived):
    block = out_ref.shape[0] // PIECES
    copies = []
    for piece in range(PIECES):
        part = (slice(None), slice(piece * block, (piece + 1) * block))
        copies.append(pltpu.make_async_copy(cache_hbm.at[part], cache_ref.at[part], arrived.at[piece]))
        copies[-1].start()
    total, spots = query.shape[0], delta_ref.shape[0]
    pick = lax.broadcasted_iota(jnp.int32, (total, spots), 1) == place_ref[...]
    pick = jnp.where(pick, 1.0, 0.0).astype(BF16)
    mine = jnp.dot(pick, delta_ref[...], preferred_element_type=F32)
    vector = frozen_ref[...].astype(F32) + LOWRANK_SCALE * mine
    query[...] = vector.astype(BF16).astype(F32)
    for piece in range(PIECES):
        copies[piece].wait()
        decode_rows(piece * block, block, length_ref, cache_ref, new_ref, out_ref, query)


def decode_rows(base, block, length_ref, cache_ref, new_ref, out_ref, query):
    span, width = cache_ref.shape[3], cache_ref.shape[4]
    heads = out_ref.shape[1] // width
    inverse = 1.0 / math.sqrt(width)
    column = lax.broadcasted_iota(jnp.int32, (8, 8 * span), 1)
    first = lax.broadcasted_iota(jnp.int32, (8, 8 * span), 0) * span
    starts = range(base, base + block, 8)
    new = new_ref[:, base : base + block, :].astype(F32)
    stack = lambda value: jnp.concatenate([value] * heads, axis=0)
    rows, scores, valid = [], [], []
    for low in starts:
        piece = query[low : low + 8, :]
        piece = jnp.concatenate([piece[:, h * width : (h + 1) * width] for h in range(heads)], axis=0)
        keys = cache_ref[0, low : low + 8, 0].reshape(8 * span, width)
        rows.append(piece)
        scores.append(
            lax.dot_general(piece.astype(BF16), keys, (((1,), (1,)), ((), ())), preferred_element_type=F32)
        )
    probs, own_probs = [], []
    for i, low in enumerate(starts):
        length = length_ref[low : low + 8, :]
        valid = (column >= first) & (column < first + length)
        bias = stack(jnp.where(valid, 0.0, -1e30))
        score = scores[i] * inverse + bias
        own = jnp.sum(rows[i] * stack(new[0, 8 * i : 8 * i + 8]), axis=1, keepdims=True) * inverse
        peak = jnp.maximum(jnp.max(score, axis=1, keepdims=True), own)
        weights = jnp.exp(score - peak)
        own_weight = jnp.exp(own - peak)
        scale = 1.0 / (jnp.sum(weights, axis=1, keepdims=True) + own_weight)
        probs.append((weights * scale).astype(BF16))
        own_probs.append((own_weight * scale).astype(BF16).astype(F32))
    mixed = []
    for i, low in enumerate(starts):
        values = cache_ref[1, low : low + 8, 0].reshape(8 * span, width)
        new_value = stack(new[1, 8 * i : 8 * i + 8])
        mixed.append(jnp.dot(probs[i], values, preferred_element_type=F32) + own_probs[i] * new_value)
    for h in range(heads):
        part = jnp.concatenate([value[8 * h : 8 * h + 8] for value in mixed], axis=0)
        out_ref[base : base + block, h * width : (h + 1) * width] = part.astype(BF16)


def decode(place, length, delta, frozen, kv_cache, new_kv):
    vmem = pl.BlockSpec(memory_space=pltpu.VMEM)
    kv_cache = pltpu.with_memory_space_constraint(kv_cache, pltpu.HBM)
    return pl.pallas_call(
        decode_kernel,
        in_specs=[vmem] * 4 + [pl.BlockSpec(memory_space=pltpu.HBM), vmem],
        out_specs=vmem,
        out_shape=jax.ShapeDtypeStruct(frozen.shape, BF16),
        scratch_shapes=[
            pltpu.VMEM(frozen.shape, F32),
            pltpu.VMEM(kv_cache.shape, BF16),
            pltpu.SemaphoreType.DMA((PIECES,)),
        ],
        compiler_params=pltpu.CompilerParams(vmem_limit_bytes=32 * 1024 * 1024),
    )(place[:, None], length[:, None], delta, frozen, kv_cache, new_kv[:, :, 0])


def shards(
    grad_a_parts,
    grad_b_parts,
    adapter_a,
    adapter_b,
    moment_a,
    moment_b,
    second_a,
    second_b,
    group_policy,
    row_slot,
    cache_length,
    features,
    frozen_query_output,
    kv_cache,
    new_kv,
):
    z, y = lax.axis_index("z"), lax.axis_index("y")
    rows, width = features.shape
    rank = grad_b_parts.shape[2]
    policies = group_policy.shape[0]
    flip = lambda value: jnp.swapaxes(value, -1, -2)

    ring_a = Ring(flip(grad_a_parts[0]).reshape(NZ, NY, rank, width), "z", 0)
    ring_b = Ring(grad_b_parts[0].reshape(NZ, NY, rank, grad_b_parts.shape[3]), "y", 1)
    go_a = ring_a.first()
    go_b = after(ring_b.first(), *go_a)
    come_a, come_b = ring_a.send(*go_a), ring_b.send(*go_b)
    (row_slot,) = after((row_slot,), *go_b)

    my_policies = lax.dynamic_index_in_dim(group_policy, z * NY + y, 0, keepdims=False)
    slot_onehot = row_slot[:, None] == jnp.arange(my_policies.shape[0])[None, :]
    row_policy = jnp.sum(jnp.where(slot_onehot, my_policies[None, :], 0), axis=1)
    before = jnp.sum((row_slot[None, :] < row_slot[:, None]).astype(jnp.int32), axis=1)
    place = row_policy * CAP + jnp.arange(rows, dtype=jnp.int32) - before
    select = (jnp.arange(policies * CAP, dtype=jnp.int32)[:, None] == place[None, :]).astype(BF16)

    packed = jnp.dot(select, features, preferred_element_type=F32).astype(BF16)

    come_a = after(come_a, packed)
    go_a = ring_a.step(*come_a)
    come_a = ring_a.send(*go_a)
    (packed,) = after((packed,), *go_a)
    feats = lax.all_to_all(packed.reshape(policies, CAP, width), ("z", "y"), 0, 0)
    go_b = ring_b.step(*after(come_b, packed))
    come_b = ring_b.send(*go_b)
    go_a = ring_a.step(*after(come_a, *go_b))
    come_a = ring_a.send(*go_a)
    *come_a, feats = tied(*come_a, feats)
    go_a = ring_a.step(*come_a)
    come_a = ring_a.send(*go_a)
    sum_b = ring_b.total(*after(come_b, *go_a))
    grad_b = swapped_sum(sum_b, "z")
    grad_a, _ = sent_sum(ring_a.total(*after(come_a, sum_b)), "y")
    feats = feats.reshape(policies * CAP, width)

    state_a = [flip(value[0]) for value in (adapter_a, moment_a, second_a)] + [grad_a]
    page_a = adamw(*state_a)[0].astype(BF16)
    partial = lax.dot_general(page_a, feats, (((1,), (1,)), ((), ())), preferred_element_type=F32)
    shrink, new_a, new_moment_a, new_second_a = tensor_sum(partial, state_a)

    state_b = [value[0] for value in (adapter_b, moment_b, second_b)] + [grad_b]
    page_b = adamw(*state_b)[0].astype(BF16)
    delta = lax.dot_general(
        shrink, page_b, (((0,), (0,)), ((), ())), preferred_element_type=F32
    ).astype(BF16)
    new_b, new_moment_b, new_second_b = adamw(*after(state_b, delta))
    delta = lax.all_to_all(delta.reshape(policies, CAP, -1), ("z", "y"), 0, 0)
    delta = delta.reshape(policies * CAP, -1)
    attended = decode(place, cache_length, delta, frozen_query_output, kv_cache, new_kv)
    return (
        flip(new_a)[None],
        new_b[None],
        flip(new_moment_a)[None],
        new_moment_b[None],
        flip(new_second_a)[None],
        new_second_b[None],
        attended,
    )


def solution(mesh):
    fine = Mesh(mesh.devices.reshape(NZ, NY, NX, NC), ("z", "y", "x", "c"))
    dp, tensor = ("z", "y"), ("x", "c")
    adapter_a, adapter_b = P(dp, tensor, None), P(dp, None, tensor)
    return jax.shard_map(
        shards,
        mesh=fine,
        in_specs=(
            P(dp, None, tensor, None),
            P(dp, None, None, tensor),
            adapter_a,
            adapter_b,
            adapter_a,
            adapter_b,
            adapter_a,
            adapter_b,
            P(),
            P(dp),
            P(dp),
            P(dp, tensor),
            P(dp, tensor),
            P(None, dp, tensor, None, None),
            P(None, dp, tensor, None),
        ),
        out_specs=(adapter_a, adapter_b, adapter_a, adapter_b, adapter_a, adapter_b, P(dp, tensor)),
        check_vma=False,
    )
```
